512 devices in a mesh: tm: 32 (over y_lo, z), tensor: 16 (over x, y_hi, core).
Axes of the slice: x: 4, y: 8 (y_hi: 2, y_lo: 4; y = y_hi * 4 + y_lo), z: 8, core: 2. Of those that a mesh axis runs over, the one named last changes fastest.
Arguments:
- tokens: bfloat16 [64, 256, 4096], P('tm'), may hold values from -200 to 200
- norm_gain: float32 [4096], replicated, may hold values from 0.1 to 1.9
- q_gain: float32 [32, 128], P('tensor'), may hold values from 0.5 to 2
- k_gain: float32 [32, 128], P('tensor'), may hold values from 0.5 to 2
- w_qkv: bfloat16 [3, 4096, 4096], P(None, 'tm', 'tensor'), may hold values from -0.09375 to 0.09375
- w_out: bfloat16 [4096, 4096], P('tensor', 'tm'), may hold values from -0.1875 to 0.1875
Outputs:
- mixed: bfloat16 [64, 256, 4096], P('tm', None, 'tensor')
The draws below stay inside these ranges and needn't reach their ends.
All inputs are finite; a program needn't handle non-finite values.
Results may differ from the reference program's by a relative error of at most 0.018.
Values may be sent and summed in bfloat16 or wider, within the bound.
A program may use at most 64 MiB of HBM per device.

```python
import math
import jax
import jax.numpy as jnp
from jax import lax

D = 4096
HEADS = 32
HD = 128
FRAMES = 16
FR_DEV = 2
P_SIZE = 256
N_TM = 32
N_TENSOR = 16


def draw_tokens(key, part):
    key = jax.random.fold_in(key, 11)
    first, second, third = jax.random.split(key, 3)
    shape = (FR_DEV * N_TM, P_SIZE, D)
    row_scale = jnp.exp(jax.random.uniform(first, (FR_DEV * N_TM, P_SIZE, 1), jnp.float32, 0.0, math.log(10.0)))
    base = jnp.clip(jax.random.normal(third, shape, jnp.float32), -4.0, 4.0)
    col_scale = jnp.exp(jax.random.uniform(second, (1, 1, D), jnp.float32, 0.0, math.log(10.0)))
    return (0.3 * base * row_scale * col_scale).astype(jnp.bfloat16)


def with_spikes(drawn, key, source, target, parts, factor):
    owner, partner = [(jnp.arange(drawn.shape[dim]) // (drawn.shape[dim] // parts)).reshape([-1 if axis == dim else 1 for axis in range(drawn.ndim)]) for dim in (source, target)]
    chosen = jax.random.permutation(key, parts)[partner]
    strong = (owner == chosen) | (owner == (partner + parts // 2) % parts)
    return jnp.where(strong, factor * drawn, drawn)


def levels(key, dims, cuts, low, top_value):
    factor_of, own = 1.0, jax.random.fold_in(key, 6)
    for dim, shards_of in cuts:
        steps = jnp.exp(jax.random.uniform(jax.random.fold_in(own, dim), (shards_of,), jnp.float32, low / len(cuts), top_value / len(cuts)))
        factor_of = factor_of * jnp.repeat(steps, dims[dim] // shards_of).reshape([-1 if axis == dim else 1 for axis in range(len(dims))])
    return factor_of


def scatter_about(stream_key, shape, spread, reach, pieces=(), held_as=jnp.bfloat16):
    level = levels(stream_key, shape, pieces, -0.22, 0.18) if pieces else 1.0
    values = jax.random.normal(stream_key, shape, jnp.float32) * spread * level
    return jnp.minimum(jnp.maximum(values, -reach), reach).astype(held_as)


def gaussian_with(rng, extent, scale, most, cuts, heavy, held_as=jnp.bfloat16):
    drawn = scale * jax.random.normal(rng, extent, jnp.float32)
    if cuts:
        drawn = drawn * levels(rng, extent, cuts, -0.22, 0.18)
    return jnp.clip(with_spikes(drawn, jax.random.fold_in(rng, 3), *heavy), -most, most).astype(held_as)


def setup_inputs(seed: int = 0) -> dict:
    arg_keys = jax.random.split(jax.random.key(seed), 7)
    tokens = draw_tokens(jax.random.fold_in(arg_keys[6], 71), 0)
    norm_gain = jnp.clip(1.0 + 0.18 * jax.random.normal(arg_keys[1], (D,), jnp.float32), 0.1, 1.9)
    q_gain = jnp.clip(jnp.exp(math.log(2.0) - 1.3862944 * jax.random.uniform(arg_keys[2], (HEADS, HD), jnp.float32) ** levels(arg_keys[2], (HEADS, HD), ((0, 16),), -0.2, 0.2)), 0.5, 2.0)
    k_gain = jnp.clip(jnp.exp(math.log(2.0) - 1.3862944 * jax.random.uniform(arg_keys[3], (HEADS, HD), jnp.float32) ** levels(arg_keys[3], (HEADS, HD), ((0, 16),), -0.2, 0.2)), 0.5, 2.0)
    w_qkv = scatter_about(arg_keys[4], (3, D, D), D ** -0.5, 0.09375, ((1, 32), (2, 16)))
    w_out = gaussian_with(arg_keys[5], (D, D), D ** -0.5, 0.1875, ((0, 16), (1, 32)), (0, 1, 32, 2.75))
    return dict(tokens=tokens, norm_gain=norm_gain, q_gain=q_gain, k_gain=k_gain, w_qkv=w_qkv, w_out=w_out)


def reference(tokens, norm_gain, q_gain, k_gain, w_qkv, w_out):
    rows_all = tokens.shape[0]
    patches = tokens.shape[1]
    width = tokens.shape[2]
    values = tokens.astype(jnp.float32)
    meansq = lax.optimization_barrier(jnp.mean(values * values, axis=-1, keepdims=True))
    normed = (values * lax.rsqrt(meansq + 1e-06) * norm_gain).astype(jnp.bfloat16)
    flat = normed.reshape(rows_all * patches, width)
    heads = q_gain.shape[0]
    head_size = q_gain.shape[1]

    def head_norm(raw, gain):
        split = raw.reshape(rows_all * patches, heads, head_size)
        scale = lax.rsqrt(lax.optimization_barrier(jnp.mean(split * split, axis=-1, keepdims=True)) + 1e-06)
        return (split * scale * gain).astype(jnp.bfloat16)
    query = head_norm(jnp.dot(flat, w_qkv[0], preferred_element_type=jnp.float32), q_gain)
    key = head_norm(jnp.dot(flat, w_qkv[1], preferred_element_type=jnp.float32), k_gain)
    value = jnp.dot(flat, w_qkv[2], preferred_element_type=jnp.float32).astype(jnp.bfloat16)
    clips = rows_all // FRAMES
    shape = (clips, FRAMES, patches, heads, head_size)
    query = query.reshape(shape).astype(jnp.float32)
    key = key.reshape(shape).astype(jnp.float32)
    value = value.reshape(shape).astype(jnp.float32)
    scores = jnp.einsum('cfphd,cgphd->cphfg', query, key) / jnp.sqrt(jnp.float32(head_size))
    frame_ids = jnp.arange(FRAMES, dtype=jnp.int32)
    causal = frame_ids[:, None] >= frame_ids[None, :]
    expo = jnp.where(causal, jnp.exp(scores), jnp.float32(0.0))
    weights = (expo / lax.optimization_barrier(jnp.sum(expo, axis=-1, keepdims=True))).astype(jnp.bfloat16)
    attended = jnp.einsum('cphfg,cgphd->cfphd', weights.astype(jnp.float32), value).astype(jnp.bfloat16)
    attended = attended.reshape(rows_all * patches, width)
    group = width // N_TENSOR
    total = jnp.zeros((rows_all * patches, width), jnp.float32)
    for index in range(N_TENSOR):
        part = jnp.dot(attended[:, index * group:(index + 1) * group], w_out[index * group:(index + 1) * group], preferred_element_type=jnp.float32)
        total = total + part.astype(jnp.bfloat16).astype(jnp.float32)
    return total.astype(jnp.bfloat16).reshape(rows_all, patches, width)
```

```python
import jax
import jax.numpy as jnp
from jax import lax
from jax.sharding import PartitionSpec as P

FRAMES = 16


def head_norm(raw, gain):
    scale = lax.rsqrt(jnp.mean(raw * raw, axis=-1, keepdims=True) + 1e-06)
    return raw * scale * gain


def attend(query, key, value):
    head_size = query.shape[-1]
    scores = jnp.einsum(
        "fphd,gphd->phfg", query, key, preferred_element_type=jnp.float32
    ) / jnp.sqrt(jnp.float32(head_size))
    frame_ids = jnp.arange(FRAMES, dtype=jnp.int32)
    causal = frame_ids[:, None] >= frame_ids[None, :]
    expo = jnp.where(causal, jnp.exp(scores), jnp.float32(0.0))
    weights = (expo / jnp.sum(expo, axis=-1, keepdims=True)).astype(jnp.bfloat16)
    attended = jnp.einsum("phfg,gphd->fphd", weights, value, preferred_element_type=jnp.float32)
    return attended.astype(jnp.bfloat16)


def body(tokens, norm_gain, q_gain, k_gain, w_qkv, w_out):
    frames_dev, patches, width = tokens.shape
    heads_dev, head_size = q_gain.shape
    local = heads_dev * head_size
    count = frames_dev * patches
    share = FRAMES // frames_dev
    clips = lax.axis_size("tm") // share
    groups = [[c * share + i for i in range(share)] for c in range(clips)]
    values = tokens.astype(jnp.float32)
    meansq = jnp.mean(values * values, axis=-1, keepdims=True)
    normed = (values * lax.rsqrt(meansq + 1e-06) * norm_gain).astype(jnp.bfloat16)
    raw = jnp.einsum(
        "tr,xrc->xtc",
        normed.reshape(count, width),
        lax.all_gather(w_qkv, "tm", axis=1, tiled=True),
        preferred_element_type=jnp.float32,
    )
    raw = raw.reshape(3, count, heads_dev, head_size)
    query = head_norm(raw[0], q_gain)
    key = head_norm(raw[1], k_gain)
    stacked = jnp.stack([query, key, raw[2]]).astype(jnp.bfloat16)
    stacked = stacked.reshape(3, frames_dev, patches, heads_dev, head_size)
    stacked = lax.all_to_all(
        stacked, "tm", split_axis=2, concat_axis=1, tiled=True, axis_index_groups=groups
    )
    mixed_heads = attend(stacked[0], stacked[1], stacked[2])
    attended = lax.all_to_all(
        mixed_heads, "tm", split_axis=0, concat_axis=1, tiled=True, axis_index_groups=groups
    )
    terms = jnp.dot(
        attended.reshape(count, local),
        lax.all_gather(w_out, "tm", axis=1, tiled=True),
        preferred_element_type=jnp.float32,
    )
    mixed = lax.psum_scatter(terms.astype(jnp.bfloat16), "tensor", scatter_dimension=1, tiled=True)
    return mixed.reshape(frames_dev, patches, -1)


def solution(mesh):
    placed = (
        P("tm", None, None),
        P(),
        P("tensor", None),
        P("tensor", None),
        P(None, "tm", "tensor"),
        P("tensor", "tm"),
    )
    return jax.shard_map(
        body, mesh=mesh, in_specs=placed, out_specs=P("tm", None, "tensor"), check_vma=False
    )
```

```python
import functools

import jax
import jax.numpy as jnp
from jax import lax
from jax.experimental import pallas as pl
from jax.experimental.pallas import tpu as pltpu
from jax.sharding import PartitionSpec as P

MESH = pl.DeviceIdType.MESH
NY, NZ, NX = 4, 8, 4
WAVES = 2
HPW = 2 // WAVES
CW = 128 * HPW
HALF = NZ // 2


def wrap(value, size):
    return lax.rem(value + size, size)


def kernel(
    tok_hbm, gain_ref, qg_ref, kg_ref, wq_ref, wout_ref, out_ref,
    tok, wbuf, wo, nbuf, xall, acc, abuf, aall, oacc,
    tok_sem, ws_z, ws_y, wr, wr_half,
    os_z, os_y, os_swap, orecv, or_half,
    xs_a, xr_a, xs_g, xr_g,
    as_a, ar_a, as_g, ar_g,
):
    t = lax.axis_index("tm")
    j = lax.axis_index("tensor")
    y, z = t // NZ, t % NZ
    x, h, c = j // 4, (j // 2) % 2, j % 2

    def tm_dev(yy, zz):
        return (yy * NZ + zz, j)

    def tensor_id(xx, hh, cc):
        return (xx * 2 + hh) * 2 + cc

    def tensor_dev(xx, hh, cc):
        return (t, tensor_id(xx, hh, cc))

    def send(src, dst, ssem, rsem, device):
        pltpu.make_async_remote_copy(
            src_ref=src, dst_ref=dst, send_sem=ssem, recv_sem=rsem,
            device_id=device, device_id_type=MESH,
        ).start()

    def await_bytes(ref, sem):
        pltpu.make_async_copy(ref, ref, sem).wait()

    swap_t, swap_j = 2 * j + t % 2, t // 2
    swap_self = jnp.logical_and(swap_t == t, swap_j == j)
    swap_other = jnp.logical_not(swap_self)

    tok_copy = pltpu.make_async_copy(tok_hbm, tok, tok_sem)
    tok_copy.start()

    for w in range(WAVES):
        for i in range(3):
            wbuf[w, t, :, i * CW:(i + 1) * CW] = wq_ref[i, :, w * CW:(w + 1) * CW]

    barrier = pltpu.get_barrier_semaphore()
    partners = [tm_dev(y, wrap(z + d, NZ)) for d in range(1, NZ)]
    partners += [tm_dev(wrap(y + d, NY), z) for d in range(1, NY)]
    partners += [tensor_dev(wrap(x + d, NX), h, c) for d in range(1, NX)]
    partners += [tensor_dev(x, 1 - h, c), tensor_dev(x, h, 1 - c)]
    for device in partners:
        pl.semaphore_signal(barrier, inc=1, device_id=device, device_id_type=MESH)

    @pl.when(swap_other)
    def _():
        pl.semaphore_signal(barrier, inc=1, device_id=(swap_t, swap_j), device_id_type=MESH)

    pl.semaphore_wait(barrier, len(partners) + swap_other.astype(jnp.int32))

    right, left = tm_dev(y, wrap(z + 1, NZ)), tm_dev(y, wrap(z + NZ - 1, NZ))

    def row_of(d):
        return wrap(y + d, NY)

    def w_block(w, b, part):
        if part is None:
            return wbuf.at[w, b]
        return wbuf.at[w, b, pl.ds(part * 64, 64)]

    def w_send_y(w):
        for d in range(1, NY):
            send(wbuf.at[w, t], wbuf.at[w, t], ws_y.at[w, d], wr.at[w, t], tm_dev(wrap(y + d, NY), z))

    def w_first(w, d):
        b = row_of(d) * NZ + z
        for way, device in ((0, right), (1, left)):
            send(wbuf.at[w, b], wbuf.at[w, b], ws_z.at[w, d, 0, way], wr.at[w, b], device)

    def w_from_y(w):
        @pl.loop(1, NY)
        def _(d):
            b = row_of(d) * NZ + z
            await_bytes(wbuf.at[w, b], wr.at[w, b])
            w_first(w, d)

    def w_pair(d, k):
        base = row_of(d) * NZ
        return base + wrap(z - k, NZ), base + wrap(z + k, NZ)

    def w_forward(w, k, then=None):
        @pl.loop(0, NY)
        def _(d):
            for way, (b, device) in enumerate(zip(w_pair(d, k), (right, left))):
                await_bytes(wbuf.at[w, b], wr.at[w, b])
                if k < HALF - 1:
                    send(wbuf.at[w, b], wbuf.at[w, b], ws_z.at[w, d, k, way], wr.at[w, b], device)
                else:
                    piece = w_block(w, b, way)
                    rsem = wr.at[w, b] if way == 0 else wr_half.at[w, row_of(d)]
                    send(piece, piece, ws_z.at[w, d, k, way], rsem, device)
            if then is not None:
                then(d)

    def w_last(w, d):
        b, _ = w_pair(d, HALF)
        await_bytes(w_block(w, b, 0), wr.at[w, b])
        await_bytes(w_block(w, b, 1), wr_half.at[w, row_of(d)])

    def multiply(w, blocks):
        @pl.loop(0, 2)
        def _(r):
            total = acc[w, pl.ds(r * 8, 8)].reshape(256, 3 * CW)
            for b in blocks:
                rows = xall[b // 2, pl.ds(r * 256, 256), pl.ds(pl.multiple_of((b % 2) * 128, 128), 128)]
                total = total + jnp.dot(rows, wbuf[w, b], preferred_element_type=jnp.float32)
            acc[w, pl.ds(r * 8, 8)] = total.reshape(8, 32, 3 * CW)

    def multiply_first(w):
        @pl.loop(0, NY // 2)
        def _(d):
            multiply(w, [row_of(2 * d) * NZ + z, row_of(2 * d + 1) * NZ + z])

    def multiply_pair(w, k):
        @pl.loop(0, NY)
        def _(d):
            multiply(w, w_pair(d, k))

    def multiply_last(w):
        @pl.loop(0, NY)
        def _(d):
            w_last(w, d)
            multiply(w, [w_pair(d, HALF)[0]])

    def o_spread(b, n):
        for d in range(1, NY):
            send(wo.at[b], wo.at[b], os_y.at[n, d], orecv.at[b], tm_dev(wrap(y + d, NY), z))

    def o_first():
        @pl.when(swap_other)
        def _():
            await_bytes(wo.at[t], orecv.at[t])

        for way, device in ((0, right), (1, left)):
            send(wo.at[t], wo.at[t], os_z.at[0, way], orecv.at[t], device)
        o_spread(t, 0)

    def o_forward(k):
        for way, (b, device) in enumerate(((y * NZ + wrap(z - k, NZ), right), (y * NZ + wrap(z + k, NZ), left))):
            await_bytes(wo.at[b], orecv.at[b])
            if k < HALF - 1:
                send(wo.at[b], wo.at[b], os_z.at[k, way], orecv.at[b], device)
            else:
                piece = wo.at[b, pl.ds(way * 128, 128)]
                rsem = orecv.at[b] if way == 0 else or_half.at[0]
                send(piece, piece, os_z.at[k, way], rsem, device)
            o_spread(b, 2 * k - 1 + way)

    def o_last():
        b = y * NZ + wrap(z + HALF, NZ)
        await_bytes(wo.at[b, pl.ds(0, 128)], orecv.at[b])
        await_bytes(wo.at[b, pl.ds(128, 128)], or_half.at[0])
        o_spread(b, 7)

    def o_all():
        @pl.loop(1, NY)
        def _(d):
            for zz in range(NZ):
                b = row_of(d) * NZ + zz
                await_bytes(wo.at[b], orecv.at[b])

    def near(first, block, index, ssem, rsem):
        devices = [tensor_dev(x, h, 1 - c)]
        if first:
            devices.append(tensor_dev(x, 1 - h, c))
        devices += [tensor_dev(wrap(x + d, NX), h, c) for d in range(1, NX)]
        for n, device in enumerate(devices):
            send(block(index), block(index), ssem(n if first else 5 + n), rsem(index), device)

    def gather_own(block, ssem, rsem):
        near(True, block, j, ssem, rsem)

    def gather_partner(block, ssem, rsem):
        other = tensor_id(x, 1 - h, c)
        await_bytes(block(other), rsem(other))
        near(False, block, other, ssem, rsem)

    def gather_x(block, ssem, rsem):
        n = 9
        for hh in (h, 1 - h):
            for d in (1, 3, 2):
                other = tensor_id(wrap(x + d, NX), hh, c)
                await_bytes(block(other), rsem(other))
                send(block(other), block(other), ssem(n), rsem(other), tensor_dev(x, h, 1 - c))
                n += 1

    def gather_sibling(block, rsem):
        @pl.loop(0, 8)
        def _(n):
            other = n * 2 + 1 - c
            await_bytes(block(other), rsem(other))

    def x_block(index):
        return xall.at[index]

    def x_ss(n):
        return xs_g.at[n]

    def x_rs(index):
        return xr_g.at[index]

    def a_tools(w):
        return (
            lambda index: aall.at[w, index],
            lambda n: as_g.at[w, n],
            lambda index: ar_g.at[w, index],
        )

    def attention(w):
        shape = (256, 256)
        fr = lax.broadcasted_iota(jnp.int32, shape, 0)
        gc = lax.broadcasted_iota(jnp.int32, shape, 1)
        mask = jnp.logical_and((fr & 15) == (gc & 15), (gc >> 4) <= (fr >> 4))
        for hd in range(HPW):
            for ph in range(2):
                def part(i):
                    lo = i * CW + hd * 128
                    return acc[w, :, ph * 16:(ph + 1) * 16, lo:lo + 128].reshape(256, 128)

                def normed(i, gains):
                    raw = part(i)
                    scale = lax.rsqrt(jnp.mean(raw * raw, axis=-1, keepdims=True) + 1e-06)
                    head = w * HPW + hd
                    return (raw * scale * gains[head:head + 1, :]).astype(jnp.bfloat16)

                query, key = normed(0, qg_ref), normed(1, kg_ref)
                value = part(2).astype(jnp.bfloat16)
                scores = lax.dot_general(
                    query, key, (((1,), (1,)), ((), ())), preferred_element_type=jnp.float32
                ) / jnp.sqrt(jnp.float32(128))
                expo = jnp.where(mask, jnp.exp(scores), jnp.float32(0.0))
                weights = (expo / jnp.sum(expo, axis=-1, keepdims=True)).astype(jnp.bfloat16)
                att = jnp.dot(weights, value, preferred_element_type=jnp.float32).astype(jnp.bfloat16)
                abuf[w, :, ph * 16:(ph + 1) * 16, hd * 128:(hd + 1) * 128] = att.reshape(16, 16, 128)
        aall[w, j, pl.ds(z * 64, 64)] = abuf[w, pl.ds(2 * z, 2)].reshape(64, CW)
        for d in range(1, NZ):
            zz = wrap(z + d, NZ)
            send(
                abuf_flat(w, zz), aall.at[w, j, pl.ds(z * 64, 64)],
                as_a.at[w, d], ar_a.at[w, z], tm_dev(y, zz),
            )

    def abuf_flat(w, zz):
        return abuf.at[w, pl.ds(2 * zz, 2)].reshape(64, CW)

    def a_pieces(w):
        for d in range(1, NZ):
            zz = wrap(z + d, NZ)
            await_bytes(aall.at[w, j, pl.ds(zz * 64, 64)], ar_a.at[w, zz])

    def project(w, index):
        lo = w * CW
        rhs = jnp.concatenate([wo[2 * index, lo:lo + CW, :], wo[2 * index + 1, lo:lo + CW, :]], axis=-1)

        @pl.loop(0, 2)
        def _(r):
            rows = pl.ds(r * 256, 256)
            oacc[rows] = oacc[rows] + jnp.dot(
                aall[w, index, rows], rhs, preferred_element_type=jnp.float32
            )

    w_send_y(0)
    w_first(0, 0)

    @pl.when(swap_other)
    def _():
        send(wout_ref, wo.at[swap_t], os_swap.at[0], orecv.at[swap_t], (swap_t, swap_j))

    @pl.when(swap_self)
    def _():
        wo[t] = wout_ref[...]

    acc[...] = jnp.zeros_like(acc)
    oacc[...] = jnp.zeros_like(oacc)

    tok_copy.wait()
    columns = pl.ds(pl.multiple_of(j * 256, 256), 256)
    gain = gain_ref[:, columns]

    @pl.loop(0, 16)
    def _(n):
        rows = pl.ds(pl.multiple_of(n * 32, 32), 32)
        values = tok[rows].astype(jnp.float32)
        meansq = jnp.mean(values * values, axis=-1, keepdims=True)
        mine = tok[rows, columns].astype(jnp.float32)
        piece = (mine * lax.rsqrt(meansq + 1e-06) * gain).astype(jnp.bfloat16)
        nbuf[n % 8, pl.ds(pl.multiple_of((n // 8) * 32, 32), 32)] = piece

    xall[j, pl.ds(z * 64, 64)] = nbuf[z]
    for d in range(1, NZ):
        zz = wrap(z + d, NZ)
        send(nbuf.at[zz], xall.at[j, pl.ds(z * 64, 64)], xs_a.at[d], xr_a.at[z], tm_dev(y, zz))

    w_from_y(0)
    o_first()

    for d in range(1, NZ):
        zz = wrap(z + d, NZ)
        await_bytes(xall.at[j, pl.ds(zz * 64, 64)], xr_a.at[zz])
    gather_own(x_block, x_ss, x_rs)

    w_forward(0, 1)
    o_forward(1)
    gather_partner(x_block, x_ss, x_rs)
    w_forward(0, 2)
    o_forward(2)
    if WAVES > 1:
        w_send_y(1)
        w_first(1, 0)
    gather_x(x_block, x_ss, x_rs)
    w_forward(0, 3)
    o_forward(3)
    if WAVES > 1:
        w_from_y(1)
    gather_sibling(x_block, x_rs)

    multiply_first(0)
    multiply_pair(0, 1)
    if WAVES > 1:
        w_forward(1, 1)
    o_last()
    multiply_pair(0, 2)
    multiply_pair(0, 3)
    if WAVES > 1:
        w_forward(1, 2)
    multiply_last(0)
    attention(0)

    if WAVES > 1:
        w_forward(1, 3)
        multiply_first(1)
        multiply_pair(1, 1)
        a_pieces(0)
        gather_own(*a_tools(0))
        multiply_pair(1, 2)
        multiply_pair(1, 3)
        gather_partner(*a_tools(0))
        multiply_last(1)
        attention(1)
        gather_x(*a_tools(0))
        o_all()
        block, ss, rs = a_tools(0)
        gather_sibling(block, rs)
        a_pieces(1)
        gather_own(*a_tools(1))

        @pl.loop(0, 16)
        def _(n):
            project(0, n)

        gather_partner(*a_tools(1))
    else:
        a_pieces(0)
        gather_own(*a_tools(0))
        gather_partner(*a_tools(0))
        o_all()

    w = WAVES - 1
    block, ss, rs = a_tools(w)
    project(w, j)
    project(w, tensor_id(x, 1 - h, c))
    gather_x(block, ss, rs)
    for hh in (h, 1 - h):
        for d in (1, 3, 2):
            project(w, tensor_id(wrap(x + d, NX), hh, c))

    @pl.loop(0, 8)
    def _(n):
        other = n * 2 + 1 - c
        await_bytes(block(other), rs(other))
        project(w, other)

    for n in range(NZ):
        part = oacc[n * 64:(n + 1) * 64].astype(jnp.bfloat16).reshape(2, 32, 256)
        out_ref[:, n * 32:(n + 1) * 32, :] = part

    for w in range(WAVES):
        for d in range(1, NY):
            await_bytes(wbuf.at[w, t], ws_y.at[w, d])

        @pl.loop(0, NY)
        def _(d):
            for way in range(2):
                for k in range(HALF - 1):
                    await_bytes(wbuf.at[w, t], ws_z.at[w, d, k, way])
                await_bytes(w_block(w, t, 0), ws_z.at[w, d, HALF - 1, way])

        for d in range(1, NZ):
            await_bytes(abuf_flat(w, z), as_a.at[w, d])

        @pl.loop(0, 15)
        def _(n):
            await_bytes(aall.at[w, 0], as_g.at[w, n])

    for way in range(2):
        for k in range(HALF - 1):
            await_bytes(wo.at[0], os_z.at[k, way])
        await_bytes(wo.at[0, pl.ds(0, 128)], os_z.at[HALF - 1, way])

    @pl.loop(0, 8)
    def _(n):
        for d in range(1, NY):
            await_bytes(wo.at[0], os_y.at[n, d])

    @pl.when(swap_other)
    def _():
        await_bytes(wout_ref, os_swap.at[0])

    for d in range(1, NZ):
        await_bytes(nbuf.at[0], xs_a.at[d])

    @pl.loop(0, 15)
    def _(n):
        await_bytes(xall.at[0], xs_g.at[n])


def body(tokens, norm_gain, q_gain, k_gain, w_qkv, w_out):
    frames_dev, patches, width = tokens.shape
    count = frames_dev * patches
    vmem = pl.BlockSpec(memory_space=pltpu.VMEM)
    dma = pltpu.SemaphoreType.DMA
    bf16, f32 = jnp.bfloat16, jnp.float32
    return pl.pallas_call(
        kernel,
        out_shape=jax.ShapeDtypeStruct((frames_dev, patches, 256), bf16),
        in_specs=[pl.BlockSpec(memory_space=pl.ANY)] + [vmem] * 5,
        out_specs=vmem,
        scratch_shapes=[
            pltpu.VMEM((count, width), bf16),
            pltpu.VMEM((WAVES, NY * NZ, 128, 3 * CW), bf16),
            pltpu.VMEM((NY * NZ, 256, 128), bf16),
            pltpu.VMEM((NZ, 64, 256), bf16),
            pltpu.VMEM((16, count, 256), bf16),
            pltpu.VMEM((WAVES, 16, 32, 3 * CW), f32),
            pltpu.VMEM((WAVES, 16, 32, CW), bf16),
            pltpu.VMEM((WAVES, 16, count, CW), bf16),
            pltpu.VMEM((count, 256), f32),
            dma, dma((WAVES, NY, HALF, 2)), dma((WAVES, NY)), dma((WAVES, NY * NZ)), dma((WAVES, NY)),
            dma((HALF, 2)), dma((8, NY)), dma((1,)), dma((NY * NZ,)), dma((1,)),
            dma((NZ,)), dma((NZ,)), dma((15,)), dma((16,)),
            dma((WAVES, NZ)), dma((WAVES, NZ)), dma((WAVES, 15)), dma((WAVES, 16)),
        ],
        compiler_params=pltpu.CompilerParams(
            collective_id=0, has_side_effects=True, vmem_limit_bytes=56 * 1024 * 1024
        ),
        cost_estimate=pl.CostEstimate(
            flops=2 * count * width * 1024, bytes_accessed=16 * 1024 * 1024, transcendentals=count * 1024
        ),
    )(
        tokens.reshape(count, width), norm_gain.reshape(1, width), q_gain, k_gain, w_qkv, w_out
    )


def solution(mesh):
    placed = (
        P("tm", None, None),
        P(),
        P("tensor", None),
        P("tensor", None),
        P(None, "tm", "tensor"),
        P("tensor", "tm"),
    )
    return jax.shard_map(
        body, mesh=mesh, in_specs=placed, out_specs=P("tm", None, "tensor"), check_vma=False
    )
```

```python
import functools

import jax
import jax.numpy as jnp
from jax import lax
from jax.experimental import pallas as pl
from jax.experimental.pallas import tpu as pltpu
from jax.sharding import PartitionSpec as P

MESH = pl.DeviceIdType.MESH
NY, NZ, NX = 4, 8, 4
WAVES = 2
HPW = 2 // WAVES
CW = 128 * HPW
HALF = NZ // 2


def wrap(value, size):
    return lax.rem(value + size, size)


def kernel(
    tok_hbm, gain_ref, qg_ref, kg_ref, wq_ref, wout_ref, out_ref,
    tok, wbuf, wo, nbuf, xall, acc, abuf, aall, oacc,
    tok_sem, ws_z, ws_y, wr, wr_half,
    os_z, os_y, os_swap, orecv, or_half,
    xs_a, xr_a, xs_g, xr_g,
    as_a, ar_a, as_g, ar_g,
):
    t = lax.axis_index("tm")
    j = lax.axis_index("tensor")
    y, z = t // NZ, t % NZ
    x, h, c = j // 4, (j // 2) % 2, j % 2

    def tm_dev(yy, zz):
        return (yy * NZ + zz, j)

    def tensor_id(xx, hh, cc):
        return (xx * 2 + hh) * 2 + cc

    def tensor_dev(xx, hh, cc):
        return (t, tensor_id(xx, hh, cc))

    def send(src, dst, ssem, rsem, device):
        pltpu.make_async_remote_copy(
            src_ref=src, dst_ref=dst, send_sem=ssem, recv_sem=rsem,
            device_id=device, device_id_type=MESH,
        ).start()

    def await_bytes(ref, sem):
        pltpu.make_async_copy(ref, ref, sem).wait()

    swap_t, swap_j = 2 * j + t % 2, t // 2
    swap_self = jnp.logical_and(swap_t == t, swap_j == j)
    swap_other = jnp.logical_not(swap_self)

    tok_copy = pltpu.make_async_copy(tok_hbm, tok, tok_sem)
    tok_copy.start()

    for w in range(WAVES):
        for i in range(3):
            wbuf[w, t, :, i * CW:(i + 1) * CW] = wq_ref[i, :, w * CW:(w + 1) * CW]

    barrier = pltpu.get_barrier_semaphore()
    partners = [tm_dev(y, wrap(z + d, NZ)) for d in range(1, NZ)]
    partners += [tm_dev(wrap(y + d, NY), z) for d in range(1, NY)]
    partners += [tensor_dev(wrap(x + d, NX), h, c) for d in range(1, NX)]
    partners += [tensor_dev(x, 1 - h, c), tensor_dev(x, h, 1 - c)]
    for device in partners:
        pl.semaphore_signal(barrier, inc=1, device_id=device, device_id_type=MESH)

    @pl.when(swap_other)
    def _():
        pl.semaphore_signal(barrier, inc=1, device_id=(swap_t, swap_j), device_id_type=MESH)

    pl.semaphore_wait(barrier, len(partners) + swap_other.astype(jnp.int32))

    right, left = tm_dev(y, wrap(z + 1, NZ)), tm_dev(y, wrap(z + NZ - 1, NZ))

    def row_of(d):
        return wrap(y + d, NY)

    def ring_pair(d, k):
        base = row_of(d) * NZ
        return base + wrap(z - k, NZ), base + wrap(z + k, NZ)

    def ring_tools(block, half, ss_y, ss_z, rs, rs_half):
        def send_y():
            for d in range(1, NY):
                send(block(t), block(t), ss_y(d), rs(t), tm_dev(wrap(y + d, NY), z))

        def first(d):
            b = row_of(d) * NZ + z
            for way, device in ((0, right), (1, left)):
                send(block(b), block(b), ss_z(d, 0, way), rs(b), device)

        def from_y():
            @pl.loop(1, NY)
            def _(d):
                b = row_of(d) * NZ + z
                await_bytes(block(b), rs(b))
                first(d)

        def forward(k):
            @pl.loop(0, NY)
            def _(d):
                for way, (b, device) in enumerate(zip(ring_pair(d, k), (right, left))):
                    await_bytes(block(b), rs(b))
                    if k < HALF - 1:
                        send(block(b), block(b), ss_z(d, k, way), rs(b), device)
                    else:
                        rsem = rs(b) if way == 0 else rs_half(row_of(d))
                        send(half(b, way), half(b, way), ss_z(d, k, way), rsem, device)

        def last(d):
            b, _ = ring_pair(d, HALF)
            await_bytes(half(b, 0), rs(b))
            await_bytes(half(b, 1), rs_half(row_of(d)))

        def sent():
            for d in range(1, NY):
                await_bytes(block(t), ss_y(d))

            @pl.loop(0, NY)
            def _(d):
                for way in range(2):
                    for k in range(HALF - 1):
                        await_bytes(block(t), ss_z(d, k, way))
                    await_bytes(half(t, 0), ss_z(d, HALF - 1, way))

        return send_y, first, from_y, forward, last, sent

    def w_tools(w):
        return ring_tools(
            lambda b: wbuf.at[w, b], lambda b, way: wbuf.at[w, b, pl.ds(way * 64, 64)],
            lambda d: ws_y.at[w, d], lambda d, k, way: ws_z.at[w, d, k, way],
            lambda b: wr.at[w, b], lambda row: wr_half.at[w, row],
        )

    w_send_y, w_first, w_from_y, w_forward, w_last, w_sent = zip(*[w_tools(w) for w in range(WAVES)])

    def o_at(b):
        return pl.ds(pl.multiple_of((b // 2) * 128, 128), 128), pl.ds(pl.multiple_of((b % 2) * 128, 128), 128)

    def o_block(b):
        return wo.at[(slice(None), *o_at(b))]

    def o_half(b, way):
        return wo.at[(way, *o_at(b))]

    def o_spread(b, n):
        for d in range(1, NY):
            send(o_block(b), o_block(b), os_y.at[n, d], orecv.at[b], tm_dev(wrap(y + d, NY), z))

    def o_first():
        @pl.when(swap_other)
        def _():
            await_bytes(o_block(t), orecv.at[t])

        for way, device in ((0, right), (1, left)):
            send(o_block(t), o_block(t), os_z.at[0, way], orecv.at[t], device)
        o_spread(t, 0)

    def o_forward(k):
        for way, (b, device) in enumerate(zip(ring_pair(0, k), (right, left))):
            await_bytes(o_block(b), orecv.at[b])
            if k < HALF - 1:
                send(o_block(b), o_block(b), os_z.at[k, way], orecv.at[b], device)
            else:
                rsem = orecv.at[b] if way == 0 else or_half.at[0]
                send(o_half(b, way), o_half(b, way), os_z.at[k, way], rsem, device)
            o_spread(b, 2 * k - 1 + way)

    def o_last():
        b, _ = ring_pair(0, HALF)
        await_bytes(o_half(b, 0), orecv.at[b])
        await_bytes(o_half(b, 1), or_half.at[0])
        o_spread(b, 7)

    def o_all():
        @pl.loop(1, NY)
        def _(d):
            for zz in range(NZ):
                b = row_of(d) * NZ + zz
                await_bytes(o_block(b), orecv.at[b])

    def o_sent():
        for way in range(2):
            for k in range(HALF - 1):
                await_bytes(o_block(t), os_z.at[k, way])
            await_bytes(o_half(t, 0), os_z.at[HALF - 1, way])

        @pl.loop(0, NZ)
        def _(n):
            for d in range(1, NY):
                await_bytes(o_block(t), os_y.at[n, d])

    def multiply(w):
        @pl.loop(0, NY)
        def _(d):
            w_last[w](d)
            row = row_of(d)
            depth = NZ * 128

            @pl.loop(0, 2)
            def _(r):
                total = jnp.dot(
                    xall[pl.ds(pl.multiple_of(r * 256, 256), 256), pl.ds(pl.multiple_of(row * depth, depth), depth)],
                    wbuf[w, pl.ds(row * NZ, NZ)].reshape(depth, 3 * CW),
                    preferred_element_type=jnp.float32,
                )
                acc[w, pl.ds(r * 8, 8)] = acc[w, pl.ds(r * 8, 8)] + total.reshape(8, 32, 3 * CW)

    def near(first, block, index, ssem, rsem):
        devices = [tensor_dev(x, h, 1 - c)]
        if first:
            devices.append(tensor_dev(x, 1 - h, c))
        devices += [tensor_dev(wrap(x + d, NX), h, c) for d in range(1, NX)]
        for n, device in enumerate(devices):
            send(block(index), block(index), ssem(n if first else 5 + n), rsem(index), device)

    def gather_own(block, ssem, rsem):
        near(True, block, j, ssem, rsem)

    def gather_partner(block, ssem, rsem):
        other = tensor_id(x, 1 - h, c)
        await_bytes(block(other), rsem(other))
        near(False, block, other, ssem, rsem)

    def gather_x(block, ssem, rsem):
        n = 9
        for hh in (h, 1 - h):
            for d in (1, 3, 2):
                other = tensor_id(wrap(x + d, NX), hh, c)
                await_bytes(block(other), rsem(other))
                send(block(other), block(other), ssem(n), rsem(other), tensor_dev(x, h, 1 - c))
                n += 1

    def gather_sibling(block, rsem):
        @pl.loop(0, 8)
        def _(n):
            other = n * 2 + 1 - c
            await_bytes(block(other), rsem(other))

    def x_rows(index, start, size):
        return xall.at[pl.ds(start, size), pl.ds(pl.multiple_of(index * 256, 256), 256)]

    def x_pieces():
        for d in range(1, NZ):
            zz = wrap(z + d, NZ)
            await_bytes(x_rows(j, zz * 64, 64), xr_a.at[zz])

    def x_block(index):
        return x_rows(index, 0, 512)

    def x_ss(n):
        return xs_g.at[n]

    def x_rs(index):
        return xr_g.at[index]

    def a_rows(w, index, start, size):
        return aall.at[w, pl.ds(start, size), pl.ds(pl.multiple_of(index * CW, CW), CW)]

    def a_tools(w):
        return (
            lambda index: a_rows(w, index, 0, 512),
            lambda n: as_g.at[w, n],
            lambda index: ar_g.at[w, index],
        )

    def attention(w):
        shape = (256, 256)
        fr = lax.broadcasted_iota(jnp.int32, shape, 0)
        gc = lax.broadcasted_iota(jnp.int32, shape, 1)
        mask = jnp.logical_and((fr & 15) == (gc & 15), (gc >> 4) <= (fr >> 4))
        for hd in range(HPW):
            for ph in range(2):
                def part(i):
                    lo = i * CW + hd * 128
                    return acc[w, :, ph * 16:(ph + 1) * 16, lo:lo + 128].reshape(256, 128)

                def normed(i, gains):
                    raw = part(i)
                    scale = lax.rsqrt(jnp.mean(raw * raw, axis=-1, keepdims=True) + 1e-06)
                    head = w * HPW + hd
                    return (raw * scale * gains[head:head + 1, :]).astype(jnp.bfloat16)

                query, key = normed(0, qg_ref), normed(1, kg_ref)
                value = part(2).astype(jnp.bfloat16)
                scores = lax.dot_general(
                    query, key, (((1,), (1,)), ((), ())), preferred_element_type=jnp.float32
                ) / jnp.sqrt(jnp.float32(128))
                expo = jnp.where(mask, jnp.exp(scores), jnp.float32(0.0))
                weights = (expo / jnp.sum(expo, axis=-1, keepdims=True)).astype(jnp.bfloat16)
                att = jnp.dot(weights, value, preferred_element_type=jnp.float32).astype(jnp.bfloat16)
                abuf[w, :, ph * 16:(ph + 1) * 16, hd * 128:(hd + 1) * 128] = att.reshape(16, 16, 128)
        aall[w, pl.ds(z * 64, 64), pl.ds(pl.multiple_of(j * CW, CW), CW)] = abuf[w, pl.ds(2 * z, 2)].reshape(64, CW)
        for d in range(1, NZ):
            zz = wrap(z + d, NZ)
            send(
                abuf_flat(w, zz), a_rows(w, j, z * 64, 64),
                as_a.at[w, d], ar_a.at[w, z], tm_dev(y, zz),
            )

    def abuf_flat(w, zz):
        return abuf.at[w, pl.ds(2 * zz, 2)].reshape(64, CW)

    def a_pieces(w):
        for d in range(1, NZ):
            zz = wrap(z + d, NZ)
            await_bytes(a_rows(w, j, zz * 64, 64), ar_a.at[w, zz])

    def project(w):
        @pl.loop(0, 2)
        def _(r):
            rows = pl.ds(pl.multiple_of(r * 256, 256), 256)
            total = jnp.dot(aall[w, rows, :], wo[w], preferred_element_type=jnp.float32)
            if w > 0:
                total = oacc[rows] + total
            oacc[rows] = total

    w_send_y[0]()
    w_first[0](0)
    w_first[1](0)

    @pl.when(swap_other)
    def _():
        send(wout_ref, o_block(swap_t), os_swap.at[0], orecv.at[swap_t], (swap_t, swap_j))

    @pl.when(swap_self)
    def _():
        wo[(slice(None), *o_at(t))] = wout_ref[...]

    acc[...] = jnp.zeros_like(acc)

    tok_copy.wait()
    columns = pl.ds(pl.multiple_of(j * 256, 256), 256)
    gain = gain_ref[:, columns]

    @pl.loop(0, 16)
    def _(n):
        rows = pl.ds(pl.multiple_of(n * 32, 32), 32)
        values = tok[rows].astype(jnp.float32)
        meansq = jnp.mean(values * values, axis=-1, keepdims=True)
        mine = tok[rows, columns].astype(jnp.float32)
        piece = (mine * lax.rsqrt(meansq + 1e-06) * gain).astype(jnp.bfloat16)
        nbuf[n % 8, pl.ds(pl.multiple_of((n // 8) * 32, 32), 32)] = piece

    xall[pl.ds(z * 64, 64), columns] = nbuf[z]
    for d in range(1, NZ):
        zz = wrap(z + d, NZ)
        send(nbuf.at[zz], x_rows(j, z * 64, 64), xs_a.at[d], xr_a.at[z], tm_dev(y, zz))

    w_from_y[0]()
    x_pieces()
    gather_own(x_block, x_ss, x_rs)
    w_forward[0](1)
    w_send_y[1]()
    w_forward[0](2)
    gather_partner(x_block, x_ss, x_rs)
    o_first()
    w_forward[0](3)
    w_from_y[1]()
    o_forward(1)
    gather_x(x_block, x_ss, x_rs)
    w_forward[1](1)
    gather_sibling(x_block, x_rs)
    o_forward(2)
    multiply(0)
    attention(0)
    w_forward[1](2)
    o_forward(3)
    a_pieces(0)
    gather_own(*a_tools(0))
    w_forward[1](3)
    o_last()
    gather_partner(*a_tools(0))
    multiply(1)
    attention(1)
    gather_x(*a_tools(0))
    a_pieces(1)
    gather_own(*a_tools(1))
    gather_sibling(a_tools(0)[0], a_tools(0)[2])
    o_all()
    project(0)
    gather_partner(*a_tools(1))
    gather_x(*a_tools(1))
    gather_sibling(a_tools(1)[0], a_tools(1)[2])
    project(1)

    for n in range(NZ):
        part = oacc[n * 64:(n + 1) * 64].astype(jnp.bfloat16).reshape(2, 32, 256)
        out_ref[:, n * 32:(n + 1) * 32, :] = part

    for w in range(WAVES):
        w_sent[w]()

        for d in range(1, NZ):
            await_bytes(abuf_flat(w, z), as_a.at[w, d])

        @pl.loop(0, 15)
        def _(n):
            await_bytes(a_rows(w, 0, 0, 512), as_g.at[w, n])

    o_sent()

    @pl.when(swap_other)
    def _():
        await_bytes(wout_ref, os_swap.at[0])

    for d in range(1, NZ):
        await_bytes(nbuf.at[0], xs_a.at[d])

    @pl.loop(0, 15)
    def _(n):
        await_bytes(x_rows(0, 0, 512), xs_g.at[n])


def body(tokens, norm_gain, q_gain, k_gain, w_qkv, w_out):
    frames_dev, patches, width = tokens.shape
    count = frames_dev * patches
    vmem = pl.BlockSpec(memory_space=pltpu.VMEM)
    dma = pltpu.SemaphoreType.DMA
    bf16, f32 = jnp.bfloat16, jnp.float32
    return pl.pallas_call(
        kernel,
        out_shape=jax.ShapeDtypeStruct((frames_dev, patches, 256), bf16),
        in_specs=[pl.BlockSpec(memory_space=pl.ANY)] + [vmem] * 5,
        out_specs=vmem,
        scratch_shapes=[
            pltpu.VMEM((count, width), bf16),
            pltpu.VMEM((WAVES, NY * NZ, 128, 3 * CW), bf16),
            pltpu.VMEM((2, 2048, 256), bf16),
            pltpu.VMEM((NZ, 64, 256), bf16),
            pltpu.VMEM((count, width), bf16),
            pltpu.VMEM((WAVES, 16, 32, 3 * CW), f32),
            pltpu.VMEM((WAVES, 16, 32, CW), bf16),
            pltpu.VMEM((WAVES, count, 16 * CW), bf16),
            pltpu.VMEM((count, 256), f32),
            dma, dma((WAVES, NY, HALF, 2)), dma((WAVES, NY)), dma((WAVES, NY * NZ)), dma((WAVES, NY)),
            dma((HALF, 2)), dma((NZ, NY)), dma((1,)), dma((NY * NZ,)), dma((1,)),
            dma((NZ,)), dma((NZ,)), dma((15,)), dma((16,)),
            dma((WAVES, NZ)), dma((WAVES, NZ)), dma((WAVES, 15)), dma((WAVES, 16)),
        ],
        compiler_params=pltpu.CompilerParams(
            collective_id=0, has_side_effects=True, vmem_limit_bytes=56 * 1024 * 1024
        ),
        cost_estimate=pl.CostEstimate(
            flops=2 * count * width * 1024, bytes_accessed=16 * 1024 * 1024, transcendentals=count * 1024
        ),
    )(
        tokens.reshape(count, width), norm_gain.reshape(1, width), q_gain, k_gain, w_qkv, w_out.reshape(2, 128, 128)
    )


def solution(mesh):
    placed = (
        P("tm", None, None),
        P(),
        P("tensor", None),
        P("tensor", None),
        P(None, "tm", "tensor"),
        P("tensor", "tm"),
    )
    return jax.shard_map(
        body, mesh=mesh, in_specs=placed, out_specs=P("tm", None, "tensor"), check_vma=False
    )
```

```python
import functools

import jax
import jax.numpy as jnp
from jax import lax
from jax.experimental import pallas as pl
from jax.experimental.pallas import tpu as pltpu
from jax.sharding import PartitionSpec as P

MESH = pl.DeviceIdType.MESH
NY, NZ, NX = 4, 8, 4
WAVES = 2
HPW = 2 // WAVES
CW = 128 * HPW
HALF = NZ // 2
SPLIT = 32


def wrap(value, size):
    return lax.rem(value + size, size)


def kernel(
    tok_hbm, gain_ref, qg_ref, kg_ref, wq_ref, wout_ref, out_ref,
    tok, wbuf, wo, nbuf, xall, acc, abuf, aall, oacc,
    tok_sem, ws_z, ws_y, wr, wr_half, vs_z, vs_y, vr, vr_half,
    os_z, os_y, os_swap, orecv, or_half,
    xs_a, xr_a, xs_g, xr_g,
    as_a, ar_a, as_g, ar_g,
):
    t = lax.axis_index("tm")
    j = lax.axis_index("tensor")
    y, z = t // NZ, t % NZ
    x, h, c = j // 4, (j // 2) % 2, j % 2

    def tm_dev(yy, zz):
        return (yy * NZ + zz, j)

    def tensor_id(xx, hh, cc):
        return (xx * 2 + hh) * 2 + cc

    def tensor_dev(xx, hh, cc):
        return (t, tensor_id(xx, hh, cc))

    def send(src, dst, ssem, rsem, device):
        pltpu.make_async_remote_copy(
            src_ref=src, dst_ref=dst, send_sem=ssem, recv_sem=rsem,
            device_id=device, device_id_type=MESH,
        ).start()

    def await_bytes(ref, sem):
        pltpu.make_async_copy(ref, ref, sem).wait()

    swap_t, swap_j = 2 * j + t % 2, t // 2
    swap_self = jnp.logical_and(swap_t == t, swap_j == j)
    swap_other = jnp.logical_not(swap_self)

    tok_copy = pltpu.make_async_copy(tok_hbm, tok, tok_sem)
    tok_copy.start()

    for w in range(WAVES):
        for i in range(3):
            wbuf[w, t, :, i * CW:(i + 1) * CW] = wq_ref[i, :, w * CW:(w + 1) * CW]

    barrier = pltpu.get_barrier_semaphore()
    partners = [tm_dev(y, wrap(z + d, NZ)) for d in range(1, NZ)]
    partners += [tm_dev(wrap(y + d, NY), z) for d in range(1, NY)]
    partners += [tensor_dev(wrap(x + d, NX), h, c) for d in range(1, NX)]
    partners += [tensor_dev(x, 1 - h, c), tensor_dev(x, h, 1 - c)]
    for device in partners:
        pl.semaphore_signal(barrier, inc=1, device_id=device, device_id_type=MESH)

    @pl.when(swap_other)
    def _():
        pl.semaphore_signal(barrier, inc=1, device_id=(swap_t, swap_j), device_id_type=MESH)

    pl.semaphore_wait(barrier, len(partners) + swap_other.astype(jnp.int32))

    right, left = tm_dev(y, wrap(z + 1, NZ)), tm_dev(y, wrap(z + NZ - 1, NZ))

    def row_of(d):
        return wrap(y + d, NY)

    def ring_pair(d, k):
        base = row_of(d) * NZ
        return base + wrap(z - k, NZ), base + wrap(z + k, NZ)

    def ring_tools(block, half, ss_y, ss_z, rs, rs_half):
        def send_y():
            for d in range(1, NY):
                send(block(t), block(t), ss_y(d), rs(t), tm_dev(wrap(y + d, NY), z))

        def first(d):
            b = row_of(d) * NZ + z
            for way, device in ((0, right), (1, left)):
                send(block(b), block(b), ss_z(d, 0, way), rs(b), device)

        def from_y():
            @pl.loop(1, NY)
            def _(d):
                b = row_of(d) * NZ + z
                await_bytes(block(b), rs(b))
                first(d)

        def forward(k):
            @pl.loop(0, NY)
            def _(d):
                for way, (b, device) in enumerate(zip(ring_pair(d, k), (right, left))):
                    await_bytes(block(b), rs(b))
                    if k < HALF - 1:
                        send(block(b), block(b), ss_z(d, k, way), rs(b), device)
                    else:
                        rsem = rs(b) if way == 0 else rs_half(row_of(d))
                        send(half(b, way), half(b, way), ss_z(d, k, way), rsem, device)

        def last(d):
            b, _ = ring_pair(d, HALF)
            await_bytes(half(b, 0), rs(b))
            await_bytes(half(b, 1), rs_half(row_of(d)))

        def sent():
            for d in range(1, NY):
                await_bytes(block(t), ss_y(d))

            @pl.loop(0, NY)
            def _(d):
                for way in range(2):
                    for k in range(HALF - 1):
                        await_bytes(block(t), ss_z(d, k, way))
                    await_bytes(half(t, 0), ss_z(d, HALF - 1, way))

        return send_y, first, from_y, forward, last, sent

    def w_tools(w):
        lo = SPLIT if w == WAVES - 1 else 0
        rows = 128 - lo
        return ring_tools(
            lambda b: wbuf.at[w, b, pl.ds(lo, rows)],
            lambda b, way: wbuf.at[w, b, pl.ds(lo + way * (rows // 2), rows // 2)],
            lambda d: ws_y.at[w, d], lambda d, k, way: ws_z.at[w, d, k, way],
            lambda b: wr.at[w, b], lambda row: wr_half.at[w, row],
        )

    def v_block(b):
        return wbuf.at[WAVES - 1, b, pl.ds(0, SPLIT)]

    def v_half(b, way):
        return wbuf.at[WAVES - 1, b, pl.ds(way * (SPLIT // 2), SPLIT // 2)]

    def v_spread(b, n):
        for d in range(1, NY):
            send(v_block(b), v_block(b), vs_y.at[n, d], vr.at[b], tm_dev(wrap(y + d, NY), z))

    def v_first():
        for way, device in ((0, right), (1, left)):
            send(v_block(t), v_block(t), vs_z.at[0, way], vr.at[t], device)
        v_spread(t, 0)

    def v_forward(k):
        for way, (b, device) in enumerate(zip(ring_pair(0, k), (right, left))):
            await_bytes(v_block(b), vr.at[b])
            if k < HALF - 1:
                send(v_block(b), v_block(b), vs_z.at[k, way], vr.at[b], device)
            else:
                rsem = vr.at[b] if way == 0 else vr_half.at[0]
                send(v_half(b, way), v_half(b, way), vs_z.at[k, way], rsem, device)
            v_spread(b, 2 * k - 1 + way)

    def v_last():
        b, _ = ring_pair(0, HALF)
        await_bytes(v_half(b, 0), vr.at[b])
        await_bytes(v_half(b, 1), vr_half.at[0])
        v_spread(b, 7)

    def v_all():
        @pl.loop(1, NY)
        def _(d):
            for zz in range(NZ):
                b = row_of(d) * NZ + zz
                await_bytes(v_block(b), vr.at[b])

    def v_sent():
        for way in range(2):
            for k in range(HALF - 1):
                await_bytes(v_block(t), vs_z.at[k, way])
            await_bytes(v_half(t, 0), vs_z.at[HALF - 1, way])

        @pl.loop(0, NZ)
        def _(n):
            for d in range(1, NY):
                await_bytes(v_block(t), vs_y.at[n, d])

    w_send_y, w_first, w_from_y, w_forward, w_last, w_sent = zip(*[w_tools(w) for w in range(WAVES)])

    def o_at(b):
        return pl.ds(pl.multiple_of((b // 2) * 128, 128), 128), pl.ds(pl.multiple_of((b % 2) * 128, 128), 128)

    def o_block(b):
        return wo.at[(slice(None), *o_at(b))]

    o_send_y, o_first, o_from_y, o_forward, o_last, o_sent = ring_tools(
        o_block, lambda b, way: wo.at[(way, *o_at(b))],
        lambda d: os_y.at[d], lambda d, k, way: os_z.at[d, k, way],
        lambda b: orecv.at[b], lambda row: or_half.at[row],
    )

    def o_swapped():
        @pl.when(swap_other)
        def _():
            await_bytes(o_block(t), orecv.at[t])

    def o_all():
        @pl.loop(0, NY)
        def _(d):
            o_last(d)

    def multiply(w):
        @pl.loop(0, NY)
        def _(d):
            w_last[w](d)
            row = row_of(d)
            depth = NZ * 128

            total = jnp.dot(
                xall[:, pl.ds(pl.multiple_of(row * depth, depth), depth)],
                wbuf[w, pl.ds(row * NZ, NZ)].reshape(depth, 3 * CW),
                preferred_element_type=jnp.float32,
            )
            acc[w] = acc[w] + total.reshape(16, 32, 3 * CW)

    def near(first, block, index, ssem, rsem):
        devices = [tensor_dev(x, h, 1 - c)]
        if first:
            devices.append(tensor_dev(x, 1 - h, c))
        devices += [tensor_dev(wrap(x + d, NX), h, c) for d in range(1, NX)]
        for n, device in enumerate(devices):
            send(block(index), block(index), ssem(n if first else 5 + n), rsem(index), device)

    def gather_own(block, ssem, rsem):
        near(True, block, j, ssem, rsem)

    def gather_partner(block, ssem, rsem):
        other = tensor_id(x, 1 - h, c)
        await_bytes(block(other), rsem(other))
        near(False, block, other, ssem, rsem)

    def gather_x(block, ssem, rsem):
        n = 9
        for hh in (h, 1 - h):
            for d in (1, 3, 2):
                other = tensor_id(wrap(x + d, NX), hh, c)
                await_bytes(block(other), rsem(other))
                send(block(other), block(other), ssem(n), rsem(other), tensor_dev(x, h, 1 - c))
                n += 1

    def gather_sibling(block, rsem):
        @pl.loop(0, 8)
        def _(n):
            other = n * 2 + 1 - c
            await_bytes(block(other), rsem(other))

    def x_rows(index, start, size):
        return xall.at[pl.ds(start, size), pl.ds(pl.multiple_of(index * 256, 256), 256)]

    def x_pieces():
        for d in range(1, NZ):
            zz = wrap(z + d, NZ)
            await_bytes(x_rows(j, zz * 64, 64), xr_a.at[zz])

    def x_block(index):
        return x_rows(index, 0, 512)

    def x_ss(n):
        return xs_g.at[n]

    def x_rs(index):
        return xr_g.at[index]

    def a_rows(w, index, start, size):
        return aall.at[w, pl.ds(start, size), pl.ds(pl.multiple_of(index * CW, CW), CW)]

    def a_tools(w):
        return (
            lambda index: a_rows(w, index, 0, 512),
            lambda n: as_g.at[w, n],
            lambda index: ar_g.at[w, index],
        )

    def attention(w):
        shape = (256, 256)
        fr = lax.broadcasted_iota(jnp.int32, shape, 0)
        gc = lax.broadcasted_iota(jnp.int32, shape, 1)
        mask = jnp.logical_and((fr & 15) == (gc & 15), (gc >> 4) <= (fr >> 4))
        for hd in range(HPW):
            for ph in range(2):
                def part(i):
                    lo = i * CW + hd * 128
                    return acc[w, :, ph * 16:(ph + 1) * 16, lo:lo + 128].reshape(256, 128)

                def normed(i, gains):
                    raw = part(i)
                    scale = lax.rsqrt(jnp.mean(raw * raw, axis=-1, keepdims=True) + 1e-06)
                    head = w * HPW + hd
                    return (raw * scale * gains[head:head + 1, :]).astype(jnp.bfloat16)

                query, key = normed(0, qg_ref), normed(1, kg_ref)
                value = part(2).astype(jnp.bfloat16)
                scores = lax.dot_general(
                    query, key, (((1,), (1,)), ((), ())), preferred_element_type=jnp.float32
                ) / jnp.sqrt(jnp.float32(128))
                expo = jnp.where(mask, jnp.exp(scores), jnp.float32(0.0))
                weights = (expo / jnp.sum(expo, axis=-1, keepdims=True)).astype(jnp.bfloat16)
                att = jnp.dot(weights, value, preferred_element_type=jnp.float32).astype(jnp.bfloat16)
                abuf[w, :, ph * 16:(ph + 1) * 16, hd * 128:(hd + 1) * 128] = att.reshape(16, 16, 128)
        aall[w, pl.ds(z * 64, 64), pl.ds(pl.multiple_of(j * CW, CW), CW)] = abuf[w, pl.ds(2 * z, 2)].reshape(64, CW)
        for d in range(1, NZ):
            zz = wrap(z + d, NZ)
            send(
                abuf_flat(w, zz), a_rows(w, j, z * 64, 64),
                as_a.at[w, d], ar_a.at[w, z], tm_dev(y, zz),
            )

    def abuf_flat(w, zz):
        return abuf.at[w, pl.ds(2 * zz, 2)].reshape(64, CW)

    def a_pieces(w):
        for d in range(1, NZ):
            zz = wrap(z + d, NZ)
            await_bytes(a_rows(w, j, zz * 64, 64), ar_a.at[w, zz])

    def project(w):
        @pl.loop(0, 2)
        def _(r):
            rows = pl.ds(pl.multiple_of(r * 256, 256), 256)
            total = jnp.dot(aall[w, rows, :], wo[w], preferred_element_type=jnp.float32)
            if w > 0:
                total = oacc[rows] + total
            oacc[rows] = total

    w_send_y[0]()
    w_first[0](0)
    w_first[1](0)

    @pl.when(swap_other)
    def _():
        send(wout_ref, o_block(swap_t), os_swap.at[0], orecv.at[swap_t], (swap_t, swap_j))

    @pl.when(swap_self)
    def _():
        wo[(slice(None), *o_at(t))] = wout_ref[...]

    acc[...] = jnp.zeros_like(acc)

    tok_copy.wait()
    columns = pl.ds(pl.multiple_of(j * 256, 256), 256)
    gain = gain_ref[:, columns]

    @pl.loop(0, 16)
    def _(n):
        rows = pl.ds(pl.multiple_of(n * 32, 32), 32)
        values = tok[rows].astype(jnp.float32)
        meansq = jnp.mean(values * values, axis=-1, keepdims=True)
        mine = tok[rows, columns].astype(jnp.float32)
        piece = (mine * lax.rsqrt(meansq + 1e-06) * gain).astype(jnp.bfloat16)
        nbuf[n % 8, pl.ds(pl.multiple_of((n // 8) * 32, 32), 32)] = piece

    xall[pl.ds(z * 64, 64), columns] = nbuf[z]
    for d in range(1, NZ):
        zz = wrap(z + d, NZ)
        send(nbuf.at[zz], x_rows(j, z * 64, 64), xs_a.at[d], xr_a.at[z], tm_dev(y, zz))

    w_from_y[0]()
    v_first()
    x_pieces()
    gather_own(x_block, x_ss, x_rs)
    w_forward[0](1)
    gather_partner(x_block, x_ss, x_rs)
    w_send_y[1]()
    v_forward(1)
    w_forward[0](2)
    v_forward(2)
    w_forward[0](3)
    w_from_y[1]()
    v_forward(3)
    gather_x(x_block, x_ss, x_rs)
    gather_sibling(x_block, x_rs)
    multiply(0)
    attention(0)
    w_forward[1](1)
    v_last()
    o_swapped()
    o_send_y()
    w_forward[1](2)
    a_pieces(0)
    gather_own(*a_tools(0))
    w_forward[1](3)
    o_first(0)
    o_from_y()
    v_all()
    gather_partner(*a_tools(0))
    multiply(1)
    attention(1)
    o_forward(1)
    a_pieces(1)
    gather_own(*a_tools(1))
    gather_x(*a_tools(0))
    o_forward(2)
    gather_partner(*a_tools(1))
    gather_sibling(a_tools(0)[0], a_tools(0)[2])
    o_forward(3)
    o_all()
    project(0)
    gather_x(*a_tools(1))
    gather_sibling(a_tools(1)[0], a_tools(1)[2])
    project(1)

    for n in range(NZ):
        part = oacc[n * 64:(n + 1) * 64].astype(jnp.bfloat16).reshape(2, 32, 256)
        out_ref[:, n * 32:(n + 1) * 32, :] = part

    for w in range(WAVES):
        w_sent[w]()

        for d in range(1, NZ):
            await_bytes(abuf_flat(w, z), as_a.at[w, d])

        @pl.loop(0, 15)
        def _(n):
            await_bytes(a_rows(w, 0, 0, 512), as_g.at[w, n])

    v_sent()
    o_sent()

    @pl.when(swap_other)
    def _():
        await_bytes(wout_ref, os_swap.at[0])

    for d in range(1, NZ):
        await_bytes(nbuf.at[0], xs_a.at[d])

    @pl.loop(0, 15)
    def _(n):
        await_bytes(x_rows(0, 0, 512), xs_g.at[n])


def body(tokens, norm_gain, q_gain, k_gain, w_qkv, w_out):
    frames_dev, patches, width = tokens.shape
    count = frames_dev * patches
    vmem = pl.BlockSpec(memory_space=pltpu.VMEM)
    dma = pltpu.SemaphoreType.DMA
    bf16, f32 = jnp.bfloat16, jnp.float32
    return pl.pallas_call(
        kernel,
        out_shape=jax.ShapeDtypeStruct((frames_dev, patches, 256), bf16),
        in_specs=[pl.BlockSpec(memory_space=pl.ANY)] + [vmem] * 5,
        out_specs=vmem,
        scratch_shapes=[
            pltpu.VMEM((count, width), bf16),
            pltpu.VMEM((WAVES, NY * NZ, 128, 3 * CW), bf16),
            pltpu.VMEM((2, 2048, 256), bf16),
            pltpu.VMEM((NZ, 64, 256), bf16),
            pltpu.VMEM((count, width), bf16),
            pltpu.VMEM((WAVES, 16, 32, 3 * CW), f32),
            pltpu.VMEM((WAVES, 16, 32, CW), bf16),
            pltpu.VMEM((WAVES, count, 16 * CW), bf16),
            pltpu.VMEM((count, 256), f32),
            dma, dma((WAVES, NY, HALF, 2)), dma((WAVES, NY)), dma((WAVES, NY * NZ)), dma((WAVES, NY)),
            dma((HALF, 2)), dma((NZ, NY)), dma((NY * NZ,)), dma((1,)),
            dma((NY, HALF, 2)), dma((NY,)), dma((1,)), dma((NY * NZ,)), dma((NY,)),
            dma((NZ,)), dma((NZ,)), dma((15,)), dma((16,)),
            dma((WAVES, NZ)), dma((WAVES, NZ)), dma((WAVES, 15)), dma((WAVES, 16)),
        ],
        compiler_params=pltpu.CompilerParams(
            collective_id=0, has_side_effects=True, vmem_limit_bytes=56 * 1024 * 1024
        ),
        cost_estimate=pl.CostEstimate(
            flops=2 * count * width * 1024, bytes_accessed=16 * 1024 * 1024, transcendentals=count * 1024
        ),
    )(
        tokens.reshape(count, width), norm_gain.reshape(1, width), q_gain, k_gain, w_qkv, w_out.reshape(2, 128, 128)
    )


def solution(mesh):
    placed = (
        P("tm", None, None),
        P(),
        P("tensor", None),
        P("tensor", None),
        P(None, "tm", "tensor"),
        P("tensor", "tm"),
    )
    return jax.shard_map(
        body, mesh=mesh, in_specs=placed, out_specs=P("tm", None, "tensor"), check_vma=False
    )
```

```python
import functools

import jax
import jax.numpy as jnp
from jax import lax
from jax.experimental import pallas as pl
from jax.experimental.pallas import tpu as pltpu
from jax.sharding import PartitionSpec as P

MESH = pl.DeviceIdType.MESH
NY, NZ, NX = 4, 8, 4
WAVES = 2
HPW = 2 // WAVES
CW = 128 * HPW
HALF = NZ // 2
SPLIT = 64


def wrap(value, size):
    return lax.rem(value + size, size)


def kernel(
    tok_hbm, gain_ref, qg_ref, kg_ref, wq_ref, wout_ref, out_ref,
    tok, wbuf, wo, nbuf, xall, acc, abuf, aall, oacc,
    tok_sem, ws_z, ws_y, wr, wr_half, vs_z, vs_y, vr, vr_half,
    os_z, os_y, os_swap, orecv, or_half,
    xs_a, xr_a, xs_g, xr_g,
    as_a, ar_a, as_g, ar_g,
):
    t = lax.axis_index("tm")
    j = lax.axis_index("tensor")
    y, z = t // NZ, t % NZ
    x, h, c = j // 4, (j // 2) % 2, j % 2

    def tm_dev(yy, zz):
        return (yy * NZ + zz, j)

    def tensor_id(xx, hh, cc):
        return (xx * 2 + hh) * 2 + cc

    def tensor_dev(xx, hh, cc):
        return (t, tensor_id(xx, hh, cc))

    def send(src, dst, ssem, rsem, device):
        pltpu.make_async_remote_copy(
            src_ref=src, dst_ref=dst, send_sem=ssem, recv_sem=rsem,
            device_id=device, device_id_type=MESH,
        ).start()

    def await_bytes(ref, sem):
        pltpu.make_async_copy(ref, ref, sem).wait()

    swap_t, swap_j = 2 * j + t % 2, t // 2
    swap_self = jnp.logical_and(swap_t == t, swap_j == j)
    swap_other = jnp.logical_not(swap_self)

    tok_copy = pltpu.make_async_copy(tok_hbm, tok, tok_sem)
    tok_copy.start()

    for w in range(WAVES):
        for i in range(3):
            wbuf[w, t, :, i * CW:(i + 1) * CW] = wq_ref[i, :, w * CW:(w + 1) * CW]

    barrier = pltpu.get_barrier_semaphore()
    partners = [tm_dev(y, wrap(z + d, NZ)) for d in range(1, NZ)]
    partners += [tm_dev(wrap(y + d, NY), z) for d in range(1, NY)]
    partners += [tensor_dev(wrap(x + d, NX), h, c) for d in range(1, NX)]
    partners += [tensor_dev(x, 1 - h, c), tensor_dev(x, h, 1 - c)]
    for device in partners:
        pl.semaphore_signal(barrier, inc=1, device_id=device, device_id_type=MESH)

    @pl.when(swap_other)
    def _():
        pl.semaphore_signal(barrier, inc=1, device_id=(swap_t, swap_j), device_id_type=MESH)

    pl.semaphore_wait(barrier, len(partners) + swap_other.astype(jnp.int32))

    right, left = tm_dev(y, wrap(z + 1, NZ)), tm_dev(y, wrap(z + NZ - 1, NZ))

    def row_of(d):
        return wrap(y + d, NY)

    def ring_pair(d, k):
        base = row_of(d) * NZ
        return base + wrap(z - k, NZ), base + wrap(z + k, NZ)

    def ring_tools(block, half, ss_y, ss_z, rs, rs_half):
        def send_y():
            for d in range(1, NY):
                send(block(t), block(t), ss_y(d), rs(t), tm_dev(wrap(y + d, NY), z))

        def first(d):
            b = row_of(d) * NZ + z
            for way, device in ((0, right), (1, left)):
                send(block(b), block(b), ss_z(d, 0, way), rs(b), device)

        def from_y():
            @pl.loop(1, NY)
            def _(d):
                b = row_of(d) * NZ + z
                await_bytes(block(b), rs(b))
                first(d)

        def forward(k):
            @pl.loop(0, NY)
            def _(d):
                for way, (b, device) in enumerate(zip(ring_pair(d, k), (right, left))):
                    await_bytes(block(b), rs(b))
                    if k < HALF - 1:
                        send(block(b), block(b), ss_z(d, k, way), rs(b), device)
                    else:
                        rsem = rs(b) if way == 0 else rs_half(row_of(d))
                        send(half(b, way), half(b, way), ss_z(d, k, way), rsem, device)

        def last(d):
            b, _ = ring_pair(d, HALF)
            await_bytes(half(b, 0), rs(b))
            await_bytes(half(b, 1), rs_half(row_of(d)))

        def sent():
            for d in range(1, NY):
                await_bytes(block(t), ss_y(d))

            @pl.loop(0, NY)
            def _(d):
                for way in range(2):
                    for k in range(HALF - 1):
                        await_bytes(block(t), ss_z(d, k, way))
                    await_bytes(half(t, 0), ss_z(d, HALF - 1, way))

        return send_y, first, from_y, forward, last, sent

    def w_tools(w):
        lo = SPLIT if w == WAVES - 1 else 0
        rows = 128 - lo
        return ring_tools(
            lambda b: wbuf.at[w, b, pl.ds(lo, rows)],
            lambda b, way: wbuf.at[w, b, pl.ds(lo + way * (rows // 2), rows // 2)],
            lambda d: ws_y.at[w, d], lambda d, k, way: ws_z.at[w, d, k, way],
            lambda b: wr.at[w, b], lambda row: wr_half.at[w, row],
        )

    def v_block(b):
        return wbuf.at[WAVES - 1, b, pl.ds(0, SPLIT)]

    def v_half(b, way):
        return wbuf.at[WAVES - 1, b, pl.ds(way * (SPLIT // 2), SPLIT // 2)]

    far_row = jnp.where(y == 1, NY - 1, 0)
    relays = jnp.logical_or(y == 1, y == 2)

    def v_spread(b, n):
        for d in range(1, NY):
            to = row_of(d)

            @pl.when(jnp.logical_or(relays, to + y != NY - 1))
            def _():
                send(v_block(b), v_block(b), vs_y.at[n, d], vr.at[b], tm_dev(to, z))

    def v_far(n):
        away = (n + 1) // 2
        b = far_row * NZ + wrap(z - away if n % 2 else z + away, NZ)

        @pl.when(relays)
        def _():
            await_bytes(v_block(b), vr.at[b])
            send(v_block(b), v_block(b), vs_y.at[n, 0], vr.at[b], tm_dev(NY - 1 - far_row, z))

    def v_first():
        for way, device in ((0, right), (1, left)):
            send(v_block(t), v_block(t), vs_z.at[0, way], vr.at[t], device)
        v_spread(t, 0)

    def v_forward(k):
        for way, (b, device) in enumerate(zip(ring_pair(0, k), (right, left))):
            await_bytes(v_block(b), vr.at[b])
            if k < HALF - 1:
                send(v_block(b), v_block(b), vs_z.at[k, way], vr.at[b], device)
            else:
                rsem = vr.at[b] if way == 0 else vr_half.at[0]
                send(v_half(b, way), v_half(b, way), vs_z.at[k, way], rsem, device)
            v_spread(b, 2 * k - 1 + way)

    def v_last():
        b, _ = ring_pair(0, HALF)
        await_bytes(v_half(b, 0), vr.at[b])
        await_bytes(v_half(b, 1), vr_half.at[0])
        v_spread(b, 7)

    def v_all():
        @pl.loop(1, NY)
        def _(d):
            row = row_of(d)

            @pl.when(jnp.logical_not(jnp.logical_and(relays, row == far_row)))
            def _():
                for zz in range(NZ):
                    b = row * NZ + zz
                    await_bytes(v_block(b), vr.at[b])

    def v_sent():
        for way in range(2):
            for k in range(HALF - 1):
                await_bytes(v_block(t), vs_z.at[k, way])
            await_bytes(v_half(t, 0), vs_z.at[HALF - 1, way])

        @pl.loop(0, NZ)
        def _(n):
            for d in range(1, NY):
                @pl.when(jnp.logical_or(relays, row_of(d) + y != NY - 1))
                def _():
                    await_bytes(v_block(t), vs_y.at[n, d])

            @pl.when(relays)
            def _():
                await_bytes(v_block(t), vs_y.at[n, 0])

    w_send_y, w_first, w_from_y, w_forward, w_last, w_sent = zip(*[w_tools(w) for w in range(WAVES)])

    def o_at(b):
        return pl.ds(pl.multiple_of((b // 2) * 128, 128), 128), pl.ds(pl.multiple_of((b % 2) * 128, 128), 128)

    def o_block(b):
        return wo.at[(slice(None), *o_at(b))]

    o_send_y, o_first, o_from_y, o_forward, o_last, o_sent = ring_tools(
        o_block, lambda b, way: wo.at[(way, *o_at(b))],
        lambda d: os_y.at[d], lambda d, k, way: os_z.at[d, k, way],
        lambda b: orecv.at[b], lambda row: or_half.at[row],
    )

    def o_swapped():
        @pl.when(swap_other)
        def _():
            await_bytes(o_block(t), orecv.at[t])

    def o_all():
        @pl.loop(0, NY)
        def _(d):
            o_last(d)

    def multiply(w):
        @pl.loop(0, NY)
        def _(d):
            w_last[w](d)
            row = row_of(d)
            depth = NZ * 128

            total = jnp.dot(
                xall[:, pl.ds(pl.multiple_of(row * depth, depth), depth)],
                wbuf[w, pl.ds(row * NZ, NZ)].reshape(depth, 3 * CW),
                preferred_element_type=jnp.float32,
            )
            acc[w] = acc[w] + total.reshape(16, 32, 3 * CW)

    def multiply_half(w, late):
        @pl.loop(0, NY)
        def _(d):
            if late:
                w_last[w](d)
            near = z // HALF
            start = row_of(d) * NZ + HALF * (1 - near if late else near)
            depth = HALF * 128

            total = jnp.dot(
                xall[:, pl.ds(pl.multiple_of(start * 128, depth), depth)],
                wbuf[w, pl.ds(start, HALF)].reshape(depth, 3 * CW),
                preferred_element_type=jnp.float32,
            )
            acc[w] = acc[w] + total.reshape(16, 32, 3 * CW)

    def near(first, block, index, ssem, rsem):
        devices = [tensor_dev(x, h, 1 - c)]
        if first:
            devices.append(tensor_dev(x, 1 - h, c))
        devices += [tensor_dev(wrap(x + d, NX), h, c) for d in range(1, NX)]
        for n, device in enumerate(devices):
            send(block(index), block(index), ssem(n if first else 5 + n), rsem(index), device)

    def gather_own(block, ssem, rsem):
        near(True, block, j, ssem, rsem)

    def gather_partner(block, ssem, rsem):
        other = tensor_id(x, 1 - h, c)
        await_bytes(block(other), rsem(other))
        near(False, block, other, ssem, rsem)

    def gather_x(block, ssem, rsem):
        n = 9
        for hh in (h, 1 - h):
            for d in (1, 3, 2):
                other = tensor_id(wrap(x + d, NX), hh, c)
                await_bytes(block(other), rsem(other))
                send(block(other), block(other), ssem(n), rsem(other), tensor_dev(x, h, 1 - c))
                n += 1

    def gather_sibling(block, rsem):
        @pl.loop(0, 8)
        def _(n):
            other = n * 2 + 1 - c
            await_bytes(block(other), rsem(other))

    def x_rows(index, start, size):
        return xall.at[pl.ds(start, size), pl.ds(pl.multiple_of(index * 256, 256), 256)]

    def x_pieces():
        for d in range(1, NZ):
            zz = wrap(z + d, NZ)
            await_bytes(x_rows(j, zz * 64, 64), xr_a.at[zz])

    def x_block(index):
        return x_rows(index, 0, 512)

    def x_ss(n):
        return xs_g.at[n]

    def x_rs(index):
        return xr_g.at[index]

    def a_rows(w, index, start, size):
        return aall.at[w, pl.ds(start, size), pl.ds(pl.multiple_of(index * CW, CW), CW)]

    def a_tools(w):
        return (
            lambda index: a_rows(w, index, 0, 512),
            lambda n: as_g.at[w, n],
            lambda index: ar_g.at[w, index],
        )

    def attention(w):
        shape = (256, 256)
        fr = lax.broadcasted_iota(jnp.int32, shape, 0)
        gc = lax.broadcasted_iota(jnp.int32, shape, 1)
        mask = jnp.logical_and((fr & 15) == (gc & 15), (gc >> 4) <= (fr >> 4))
        for hd in range(HPW):
            for ph in range(2):
                def part(i):
                    lo = i * CW + hd * 128
                    return acc[w, :, ph * 16:(ph + 1) * 16, lo:lo + 128].reshape(256, 128)

                def normed(i, gains):
                    raw = part(i)
                    scale = lax.rsqrt(jnp.mean(raw * raw, axis=-1, keepdims=True) + 1e-06)
                    head = w * HPW + hd
                    return (raw * scale * gains[head:head + 1, :]).astype(jnp.bfloat16)

                query, key = normed(0, qg_ref), normed(1, kg_ref)
                value = part(2).astype(jnp.bfloat16)
                scores = lax.dot_general(
                    query, key, (((1,), (1,)), ((), ())), preferred_element_type=jnp.float32
                ) / jnp.sqrt(jnp.float32(128))
                expo = jnp.where(mask, jnp.exp(scores), jnp.float32(0.0))
                weights = (expo / jnp.sum(expo, axis=-1, keepdims=True)).astype(jnp.bfloat16)
                att = jnp.dot(weights, value, preferred_element_type=jnp.float32).astype(jnp.bfloat16)
                abuf[w, :, ph * 16:(ph + 1) * 16, hd * 128:(hd + 1) * 128] = att.reshape(16, 16, 128)
        aall[w, pl.ds(z * 64, 64), pl.ds(pl.multiple_of(j * CW, CW), CW)] = abuf[w, pl.ds(2 * z, 2)].reshape(64, CW)
        for d in range(1, NZ):
            zz = wrap(z + d, NZ)
            send(
                abuf_flat(w, zz), a_rows(w, j, z * 64, 64),
                as_a.at[w, d], ar_a.at[w, z], tm_dev(y, zz),
            )

    def abuf_flat(w, zz):
        return abuf.at[w, pl.ds(2 * zz, 2)].reshape(64, CW)

    def a_pieces(w):
        for d in range(1, NZ):
            zz = wrap(z + d, NZ)
            await_bytes(a_rows(w, j, zz * 64, 64), ar_a.at[w, zz])

    def project(w):
        @pl.loop(0, 2)
        def _(r):
            rows = pl.ds(pl.multiple_of(r * 256, 256), 256)
            total = jnp.dot(aall[w, rows, :], wo[w], preferred_element_type=jnp.float32)
            if w > 0:
                total = oacc[rows] + total
            oacc[rows] = total

    w_send_y[0]()
    w_first[0](0)
    w_first[1](0)

    @pl.when(swap_other)
    def _():
        send(wout_ref, o_block(swap_t), os_swap.at[0], orecv.at[swap_t], (swap_t, swap_j))

    @pl.when(swap_self)
    def _():
        wo[(slice(None), *o_at(t))] = wout_ref[...]

    acc[...] = jnp.zeros_like(acc)

    tok_copy.wait()
    columns = pl.ds(pl.multiple_of(j * 256, 256), 256)
    gain = gain_ref[:, columns]

    @pl.loop(0, 16)
    def _(n):
        rows = pl.ds(pl.multiple_of(n * 32, 32), 32)
        values = tok[rows].astype(jnp.float32)
        meansq = jnp.mean(values * values, axis=-1, keepdims=True)
        mine = tok[rows, columns].astype(jnp.float32)
        piece = (mine * lax.rsqrt(meansq + 1e-06) * gain).astype(jnp.bfloat16)
        nbuf[n % 8, pl.ds(pl.multiple_of((n // 8) * 32, 32), 32)] = piece

    xall[pl.ds(z * 64, 64), columns] = nbuf[z]
    for d in range(1, NZ):
        zz = wrap(z + d, NZ)
        send(nbuf.at[zz], x_rows(j, z * 64, 64), xs_a.at[d], xr_a.at[z], tm_dev(y, zz))

    w_from_y[0]()
    v_first()
    x_pieces()
    gather_own(x_block, x_ss, x_rs)
    w_forward[0](1)
    gather_partner(x_block, x_ss, x_rs)
    w_send_y[1]()
    v_forward(1)
    v_far(0)
    w_forward[0](2)
    v_forward(2)
    o_swapped()
    o_send_y()
    w_forward[0](3)
    w_from_y[1]()
    v_forward(3)
    v_far(1)
    v_far(2)
    gather_x(x_block, x_ss, x_rs)
    gather_sibling(x_block, x_rs)
    multiply(0)
    attention(0)
    w_forward[1](1)
    v_far(3)
    v_far(4)
    v_last()
    a_pieces(0)
    gather_own(*a_tools(0))
    w_forward[1](2)
    v_far(5)
    v_far(6)
    v_far(7)
    w_forward[1](3)
    o_first(0)
    o_from_y()
    gather_partner(*a_tools(0))
    v_all()
    multiply_half(1, False)
    multiply_half(1, True)
    attention(1)
    o_forward(1)
    a_pieces(1)
    gather_own(*a_tools(1))
    o_forward(2)
    gather_x(*a_tools(0))
    gather_partner(*a_tools(1))
    o_forward(3)
    gather_sibling(a_tools(0)[0], a_tools(0)[2])
    o_all()
    project(0)
    gather_x(*a_tools(1))
    gather_sibling(a_tools(1)[0], a_tools(1)[2])
    project(1)

    for n in range(NZ):
        part = oacc[n * 64:(n + 1) * 64].astype(jnp.bfloat16).reshape(2, 32, 256)
        out_ref[:, n * 32:(n + 1) * 32, :] = part

    for w in range(WAVES):
        w_sent[w]()

        for d in range(1, NZ):
            await_bytes(abuf_flat(w, z), as_a.at[w, d])

        @pl.loop(0, 15)
        def _(n):
            await_bytes(a_rows(w, 0, 0, 512), as_g.at[w, n])

    v_sent()
    o_sent()

    @pl.when(swap_other)
    def _():
        await_bytes(wout_ref, os_swap.at[0])

    for d in range(1, NZ):
        await_bytes(nbuf.at[0], xs_a.at[d])

    @pl.loop(0, 15)
    def _(n):
        await_bytes(x_rows(0, 0, 512), xs_g.at[n])


def body(tokens, norm_gain, q_gain, k_gain, w_qkv, w_out):
    frames_dev, patches, width = tokens.shape
    count = frames_dev * patches
    vmem = pl.BlockSpec(memory_space=pltpu.VMEM)
    dma = pltpu.SemaphoreType.DMA
    bf16, f32 = jnp.bfloat16, jnp.float32
    return pl.pallas_call(
        kernel,
        out_shape=jax.ShapeDtypeStruct((frames_dev, patches, 256), bf16),
        in_specs=[pl.BlockSpec(memory_space=pl.ANY)] + [vmem] * 5,
        out_specs=vmem,
        scratch_shapes=[
            pltpu.VMEM((count, width), bf16),
            pltpu.VMEM((WAVES, NY * NZ, 128, 3 * CW), bf16),
            pltpu.VMEM((2, 2048, 256), bf16),
            pltpu.VMEM((NZ, 64, 256), bf16),
            pltpu.VMEM((count, width), bf16),
            pltpu.VMEM((WAVES, 16, 32, 3 * CW), f32),
            pltpu.VMEM((WAVES, 16, 32, CW), bf16),
            pltpu.VMEM((WAVES, count, 16 * CW), bf16),
            pltpu.VMEM((count, 256), f32),
            dma, dma((WAVES, NY, HALF, 2)), dma((WAVES, NY)), dma((WAVES, NY * NZ)), dma((WAVES, NY)),
            dma((HALF, 2)), dma((NZ, NY)), dma((NY * NZ,)), dma((1,)),
            dma((NY, HALF, 2)), dma((NY,)), dma((1,)), dma((NY * NZ,)), dma((NY,)),
            dma((NZ,)), dma((NZ,)), dma((15,)), dma((16,)),
            dma((WAVES, NZ)), dma((WAVES, NZ)), dma((WAVES, 15)), dma((WAVES, 16)),
        ],
        compiler_params=pltpu.CompilerParams(
            collective_id=0, has_side_effects=True, vmem_limit_bytes=56 * 1024 * 1024
        ),
        cost_estimate=pl.CostEstimate(
            flops=2 * count * width * 1024, bytes_accessed=16 * 1024 * 1024, transcendentals=count * 1024
        ),
    )(
        tokens.reshape(count, width), norm_gain.reshape(1, width), q_gain, k_gain, w_qkv, w_out.reshape(2, 128, 128)
    )


def solution(mesh):
    placed = (
        P("tm", None, None),
        P(),
        P("tensor", None),
        P("tensor", None),
        P(None, "tm", "tensor"),
        P("tensor", "tm"),
    )
    return jax.shard_map(
        body, mesh=mesh, in_specs=placed, out_specs=P("tm", None, "tensor"), check_vma=False
    )
```
